32 devices in a mesh: groups: 2 (over x), blk: 16 (over z, y, core).
Axes of the slice: x: 2, y: 2, z: 4, core: 2. Of those that a mesh axis runs over, the one named last changes fastest.
Arguments:
- embeddings: bfloat16 [16384, 1024], P(('groups', 'blk')), parts along dimension 0, may hold values from -6 to 6
- position: int32 [16384], P(('groups', 'blk')), parts along dimension 0, may hold values from 0 to 8191, as said below
- member: int32 [16384], P(('groups', 'blk')), parts along dimension 0, may hold values from 0 to 8191, as said below
- cluster: int32 [16384], P('groups'), parts along dimension 0, may hold values from 0 to 32, as said below
Outputs:
- smoothed: bfloat16 [16384, 1024], P(('groups', 'blk')), parts along dimension 0
- soft_count: bfloat16 [16384], P(('groups', 'blk')), parts along dimension 0
The draws below stay inside these ranges and needn't reach their ends.
There are 2 independent parts, one for each index of `groups`. The reference program is written for one: setup_inputs(seed, part) draws one part's arguments, and reference() takes and returns one part's arrays. A program takes and returns all parts, laid end to end along the dimension named above; each array names one. Nothing has to cross between parts.
Inputs may be any that keep to these rules, and one draw needn't show every extreme that they name: `position`: A permutation; of the rows of one device exactly 32 land in each device's range of 512 places. `member`: the inverse permutation of position. Never falls; ids are consecutive from 0; each cluster holds 1 to 1024 consecutive places and one holds exactly 1024.
All inputs are finite; a program needn't handle non-finite values.
Results may differ from the reference program's by a relative error of at most 0.0065.
Values may be sent and summed in bfloat16 or wider, within the bound.
A program may use at most 64 MiB of HBM per device.

```python
import jax
import jax.numpy as jnp
from jax import lax

D = 1024
R_DEV = 512
SPAN = 2
ROWS = 8192
MOST = 1024


PIECES = 4


def layout(key):
    first_key, second_key = jax.random.split(key)
    devices = ROWS // R_DEV
    per_peer = R_DEV // devices
    picks = jax.vmap(lambda sub: jax.random.permutation(sub, R_DEV))(jax.random.split(first_key, devices))
    slots = jax.vmap(lambda sub: jax.random.permutation(sub, R_DEV))(jax.random.split(second_key, devices))
    target = picks // per_peer
    within = picks % per_peer
    senders = jnp.arange(devices, dtype=jnp.int32)[:, None]
    local = slots[target, senders * per_peer + within]
    placed = (target * R_DEV + local).reshape(ROWS).astype(jnp.int32)
    return (placed, jnp.argsort(placed).astype(jnp.int32))


def draw_position(key, part):
    return layout(key)[0]


def draw_member(key, part):
    return layout(key)[1]


def draw_cluster(key, part):
    key = jax.random.fold_in(key, 11)
    cut_key, pick_key = jax.random.split(key)
    offset = R_DEV // 2
    windows = ROWS // MOST + 1
    window_ids = jnp.arange(windows, dtype=jnp.int32)
    starts = jnp.maximum(window_ids * MOST - offset, 0)
    ends = jnp.minimum((window_ids + 1) * MOST - offset, ROWS)
    steps = ((ends - starts) // PIECES).astype(jnp.int32)
    jitter = jax.random.randint(cut_key, (windows, PIECES - 1), 0, 1 << 30, dtype=jnp.int32) % steps[:, None]
    cuts = jnp.arange(1, PIECES, dtype=jnp.int32)[None, :] * steps[:, None] + jitter
    chosen = jax.random.randint(pick_key, (), 1, windows - 1, dtype=jnp.int32)
    places = jnp.arange(ROWS, dtype=jnp.int32)
    which = ((places + offset) // MOST).astype(jnp.int32)
    local = places - starts[which]
    inside = jnp.sum((cuts[which] <= local[:, None]).astype(jnp.int32), axis=1)
    inside = jnp.where(which == chosen, 0, inside)
    earlier = which * PIECES - (PIECES - 1) * (chosen < which).astype(jnp.int32)
    return (earlier + inside).astype(jnp.int32)


def shard_levels(own_key, dims, cuts, low, high):
    def one(dim, parts):
        draws = jax.random.uniform(jax.random.fold_in(jax.random.fold_in(own_key, 6), dim), (parts,), jnp.float32, low / len(cuts), high / len(cuts))
        return jnp.repeat(jnp.exp(draws), dims[dim] // parts).reshape((-1,) + (1,) * (len(dims) - dim - 1))

    gain = one(*cuts[0])
    for cut in cuts[1:]:
        gain = gain * one(*cut)
    return gain


def noise(stream_key, extent, spread, limit, cuts=(), kind=jnp.bfloat16):
    result = jax.random.normal(stream_key, extent, jnp.float32) * spread
    if len(cuts) > 0:
        result = shard_levels(stream_key, extent, cuts, -0.22, 0.18) * result
    return jnp.clip(result, min=-limit, max=limit).astype(kind)


def setup_inputs(seed: int = 0, part: int = 0) -> dict:
    arg_keys = jax.random.split(jax.random.key(seed), 5)
    own_keys = jax.random.split(jax.random.fold_in(arg_keys[4], part), 5)
    return {
        "embeddings": noise(own_keys[0], (ROWS, D), 1.0, 6.0, ((0, 16),)),
        "position": draw_position(jax.random.fold_in(jax.random.fold_in(arg_keys[4], part), 71), part),
        "member": draw_member(jax.random.fold_in(jax.random.fold_in(arg_keys[4], part), 71), part),
        "cluster": draw_cluster(jax.random.fold_in(jax.random.fold_in(arg_keys[4], part), 71), part),
    }


SHARPNESS = 32.0
EPSILON = 1e-06

def inverse_norm(row_block):
    widened = row_block.astype(jnp.float32)
    return lax.rsqrt(lax.optimization_barrier(jnp.sum(widened * widened, axis=1)) + EPSILON)

def reference(embeddings, position, member, cluster):
    sorted_rows = embeddings[member]
    margin = SPAN * R_DEV
    window_size = R_DEV * (2 * SPAN + 1)
    inverse = inverse_norm(sorted_rows)
    padded_rows = jnp.pad(sorted_rows, ((margin, margin), (0, 0)))
    padded_inverse = jnp.pad(inverse, (margin, margin))
    padded_ids = jnp.pad(cluster, (margin, margin), constant_values=-1)

    def one_block(block_index):
        start = (block_index * R_DEV).astype(jnp.int32)
        own_rows = lax.dynamic_slice_in_dim(sorted_rows, start, R_DEV, 0)
        own_inverse = lax.dynamic_slice_in_dim(inverse, start, R_DEV, 0)
        own_ids = lax.dynamic_slice_in_dim(cluster, start, R_DEV, 0)
        window = lax.dynamic_slice_in_dim(padded_rows, start, window_size, 0)
        window_inverse = lax.dynamic_slice_in_dim(padded_inverse, start, window_size, 0)
        window_ids = lax.dynamic_slice_in_dim(padded_ids, start, window_size, 0)
        products = jnp.dot(own_rows, window.T, preferred_element_type=jnp.float32)
        cosine = products * own_inverse[:, None] * window_inverse[None, :]
        row_places = start + jnp.arange(R_DEV, dtype=jnp.int32)
        col_places = start - margin + jnp.arange(window_size, dtype=jnp.int32)
        allowed = (own_ids[:, None] == window_ids[None, :]) & (row_places[:, None] != col_places[None, :])
        scores = jnp.where(allowed, jax.nn.sigmoid(SHARPNESS * cosine), jnp.float32(0.0))
        tallies = lax.optimization_barrier(jnp.sum(scores, axis=1))
        weights = scores.astype(jnp.bfloat16)
        totals = jnp.zeros((R_DEV, D), jnp.float32)
        for slot in range(2 * SPAN + 1):
            lower = slot * R_DEV
            term = jnp.dot(weights[:, lower:lower + R_DEV], window[lower:lower + R_DEV], preferred_element_type=jnp.float32)
            if slot != SPAN:
                term = lax.optimization_barrier(term.astype(jnp.bfloat16)).astype(jnp.float32)
            totals = totals + term
        return (totals, tallies)
    totals, tallies = lax.map(one_block, jnp.arange(ROWS // R_DEV, dtype=jnp.int32))
    totals = totals.reshape(ROWS, D)
    tallies = tallies.reshape(ROWS)
    smoothed_sorted = (totals / jnp.sqrt(1.0 + tallies)[:, None]).astype(jnp.bfloat16)
    counted_sorted = tallies.astype(jnp.bfloat16)
    return (smoothed_sorted[position], counted_sorted[position])
```

```python
import functools

import jax
import jax.numpy as jnp
from jax import lax
from jax.experimental import pallas as pl
from jax.experimental.pallas import tpu as pltpu
from jax.sharding import PartitionSpec as P

SHARPNESS = 32.0
EPSILON = 1e-06
TILE = 256
F32 = jnp.float32
BF16 = jnp.bfloat16


def snake(device, devices):
    if devices != 16:
        return device
    z, y, core = device // 4, (device // 2) % 2, device % 2
    turn = z % 2
    return z * 4 + (y + turn - 2 * y * turn) * 2 + core


def as_column(row):
    return jnp.transpose(jnp.broadcast_to(row, (128, row.shape[1])))[:, :1]


def as_row(column):
    return jnp.transpose(jnp.broadcast_to(column, (column.shape[0], 128)))[:1, :]


def ones_where(condition):
    return jnp.where(condition, 1.0, 0.0)


def kernel(
    devices, slab, emb, pos, mem, ids, out, count_out,
    outgoing, incoming, own, mate, prev, after, relayed, total, result, returning, returned,
    tallies, tally_table, send_col, place_col, own_inv, own_ids, tally, mem_in,
    mem_sems, out_send, out_recv, win_send, win_recv, back_send, back_recv, tal_send, tal_recv,
):
    rows, width = emb.shape
    slots = devices * slab
    per_peer = rows // devices
    me = lax.axis_index("blk")
    block = snake(me, devices)
    chip, core = block // 2, block % 2
    chips = devices // 2

    def dev(b):
        return {"blk": b}

    def remote(src, dst, send, recv, target):
        return pltpu.make_async_remote_copy(
            src_ref=src, dst_ref=dst, send_sem=send, recv_sem=recv,
            device_id=dev(target), device_id_type=pl.DeviceIdType.MESH,
        )

    def at_slab(ref, index):
        return ref.at[pl.ds(pl.multiple_of(index * slab, slab), slab)]

    barrier = pltpu.get_barrier_semaphore()

    @pl.loop(1, devices)
    def _(k):
        pl.semaphore_signal(
            barrier, inc=1, device_id=dev((me + k) % devices),
            device_id_type=pl.DeviceIdType.MESH,
        )

    pos_row = pos[...].astype(F32)
    pos_col = as_column(pos_row)
    rank = jnp.sum(ones_where(pos_col < pos_row), axis=0, keepdims=True)
    block_row = lax.shift_right_logical(pos[...], (rows - 1).bit_length()).astype(F32)
    send_row = rank + block_row * (slab - per_peer)
    send_col[...] = as_column(send_row)

    @pl.loop(0, slots // TILE)
    def _(t):
        start = pl.multiple_of(t * TILE, TILE)
        places = (lax.broadcasted_iota(jnp.int32, (TILE, rows), 0) + start).astype(F32)
        pick = ones_where(places == send_row).astype(BF16)
        outgoing[pl.ds(start, TILE), :] = jnp.dot(
            pick, emb[...], preferred_element_type=F32
        ).astype(BF16)

    pl.semaphore_wait(barrier, devices - 1)

    def out_copy(k):
        peer = (me + k) % devices
        return remote(
            at_slab(outgoing, snake(peer, devices)), at_slab(incoming, me),
            out_send.at[k], out_recv.at[k], peer,
        )

    def mem_copy():
        return remote(mem, mem_in, mem_sems.at[0], mem_sems.at[1], block)

    @pl.when(block != me)
    def _():
        mem_copy().start()

    @pl.loop(1, devices)
    def _(k):
        out_copy(k).start()

    at_slab(incoming, me)[...] = at_slab(outgoing, block)[...]

    @pl.when(block == me)
    def _():
        mem_in[...] = mem[...]

    @pl.when(block != me)
    def _():
        mem_copy().wait()

    src_row = lax.shift_right_logical(mem_in[...], (rows - 1).bit_length()).astype(F32)
    src_col = as_column(src_row)
    earlier = lax.broadcasted_iota(jnp.int32, (rows, rows), 0) < lax.broadcasted_iota(
        jnp.int32, (rows, rows), 1
    )
    before = jnp.sum(ones_where((src_col == src_row) & earlier), axis=0, keepdims=True)
    place_row = src_row * slab + before
    place_col[...] = as_column(place_row)
    own_ids[...] = as_column(ids[block].astype(F32))

    @pl.loop(1, devices)
    def _(k):
        out_copy(k).wait_recv()

    @pl.loop(0, rows // TILE)
    def _(t):
        part = pl.ds(pl.multiple_of(t * TILE, TILE), TILE)
        lanes = lax.broadcasted_iota(jnp.int32, (TILE, slots), 1).astype(F32)
        pick = ones_where(lanes == place_col[part, :]).astype(BF16)
        own[part, :] = jnp.dot(pick, incoming[...], preferred_element_type=F32).astype(BF16)

    mate_dev = snake(block + 1 - 2 * core, devices)
    has_prev, has_after = chip > 0, chip < chips - 1
    prev_dev = snake(jnp.maximum(block - 2, 0), devices)
    after_dev = snake(jnp.minimum(block + 2, devices - 1), devices)

    def to_mate():
        return remote(own, mate, win_send.at[0], win_recv.at[0], mate_dev)

    def to_after():
        return remote(own, prev, win_send.at[1], win_recv.at[1], after_dev)

    def to_prev():
        return remote(own, after, win_send.at[2], win_recv.at[2], prev_dev)

    def relay(source):
        return remote(source, relayed, win_send.at[3], win_recv.at[3], mate_dev)

    @pl.when(has_after)
    def _():
        to_after().start()

    @pl.when(has_prev)
    def _():
        to_prev().start()

    to_mate().start()

    def inverse(ref):
        widened = ref[...].astype(F32)
        return lax.rsqrt(jnp.sum(widened * widened, axis=1, keepdims=True) + EPSILON)

    def visit(other, other_inv_row, other_block, first):
        other_ids = ids[other_block].astype(F32)

        @pl.loop(0, rows // TILE)
        def _(t):
            start = pl.multiple_of(t * TILE, TILE)
            part = pl.ds(start, TILE)
            products = lax.dot_general(
                own[part, :], other[...], (((1,), (1,)), ((), ())), preferred_element_type=F32
            )
            half = products * (own_inv[part, :] * (0.5 * SHARPNESS)) * other_inv_row
            allowed = own_ids[part, :] == other_ids
            if first:
                here = lax.broadcasted_iota(jnp.int32, (TILE, rows), 0) + start
                there = lax.broadcasted_iota(jnp.int32, (TILE, rows), 1)
                allowed = allowed & (here != there)
            scores = jnp.where(allowed, 0.5 + 0.5 * jnp.tanh(half), 0.0)
            term = jnp.dot(scores.astype(BF16), other[...], preferred_element_type=F32)
            counted = jnp.sum(scores, axis=1, keepdims=True)
            if first:
                total[part, :] = term
                tally[part, :] = counted
            else:
                total[part, :] += term
                tally[part, :] += counted

    own_inv[...] = inverse(own)
    visit(own, as_row(own_inv[...]), block, True)
    to_mate().wait_recv()
    visit(mate, as_row(inverse(mate)), block + 1 - 2 * core, False)

    @pl.when(has_prev)
    def _():
        to_after().wait_recv()

        @pl.when(core == 1)
        def _():
            relay(prev).start()

    @pl.when(has_after)
    def _():
        to_prev().wait_recv()

        @pl.when(core == 0)
        def _():
            relay(after).start()

    @pl.when(has_prev)
    def _():
        visit(prev, as_row(inverse(prev)), block - 2, False)

    @pl.when(has_after)
    def _():
        visit(after, as_row(inverse(after)), block + 2, False)

    gets_relay = ((core == 0) & has_prev) | ((core == 1) & has_after)

    @pl.when(gets_relay)
    def _():
        relay(prev).wait_recv()
        visit(relayed, as_row(inverse(relayed)), block - 1 + 2 * core, False)

    scale = lax.rsqrt(1.0 + tally[...])
    result[...] = (total[...] * scale).astype(BF16)
    tallies[block] = as_row(tally[...])

    def tally_copy(k):
        peer = (me + k) % devices
        return remote(
            tallies.at[block], tallies.at[block], tal_send.at[k], tal_recv.at[k], peer
        )

    def back_copy(k):
        peer = (me + k) % devices
        return remote(
            at_slab(returning, peer), at_slab(returned, block),
            back_send.at[k], back_recv.at[k], peer,
        )

    @pl.loop(1, devices)
    def _(k):
        tally_copy(k).start()

    @pl.loop(0, slots // TILE)
    def _(t):
        start = pl.multiple_of(t * TILE, TILE)
        places = (lax.broadcasted_iota(jnp.int32, (TILE, rows), 0) + start).astype(F32)
        pick = ones_where(places == place_row).astype(BF16)
        returning[pl.ds(start, TILE), :] = jnp.dot(
            pick, result[...], preferred_element_type=F32
        ).astype(BF16)

    @pl.loop(1, devices)
    def _(k):
        back_copy(k).start()

    at_slab(returned, block)[...] = at_slab(returning, me)[...]

    @pl.loop(1, devices)
    def _(k):
        tally_copy(k).wait_recv()

    tally_table[...] = jnp.zeros_like(tally_table)

    @pl.loop(0, devices)
    def _(b):
        tally_table[pl.ds(b, 1), :] = tallies[b]

    which = lax.broadcasted_iota(jnp.int32, (128, rows), 0).astype(F32)
    in_block = jnp.dot(
        jnp.transpose(tally_table[...]).astype(BF16),
        ones_where(which == block_row).astype(BF16),
        preferred_element_type=F32,
    )
    inside = pos_row - block_row * rows
    lines = lax.broadcasted_iota(jnp.int32, (rows, rows), 0).astype(F32)
    count_out[...] = jnp.sum(jnp.where(lines == inside, in_block, 0.0), axis=0, keepdims=True)

    @pl.loop(1, devices)
    def _(k):
        back_copy(k).wait_recv()

    @pl.loop(0, rows // TILE)
    def _(t):
        part = pl.ds(pl.multiple_of(t * TILE, TILE), TILE)
        lanes = lax.broadcasted_iota(jnp.int32, (TILE, slots), 1).astype(F32)
        pick = ones_where(lanes == send_col[part, :]).astype(BF16)
        out[part, :] = jnp.dot(pick, returned[...], preferred_element_type=F32).astype(BF16)

    @pl.loop(1, devices)
    def _(k):
        out_copy(k).wait_send()
        tally_copy(k).wait_send()
        back_copy(k).wait_send()

    to_mate().wait_send()

    @pl.when(has_after)
    def _():
        to_after().wait_send()

    @pl.when(has_prev)
    def _():
        to_prev().wait_send()

    @pl.when(((core == 1) & has_prev) | ((core == 0) & has_after))
    def _():
        relay(prev).wait_send()


def local(embeddings, position, member, cluster):
    rows, width = embeddings.shape
    devices = lax.axis_size("blk")
    slab = max(16, rows // devices)
    slots = devices * slab
    vmem = pl.BlockSpec(memory_space=pltpu.VMEM)
    dma = pltpu.SemaphoreType.DMA
    smoothed, counts = pl.pallas_call(
        functools.partial(kernel, devices, slab),
        out_shape=(
            jax.ShapeDtypeStruct((rows, width), BF16),
            jax.ShapeDtypeStruct((1, rows), F32),
        ),
        in_specs=[vmem] * 4,
        out_specs=(vmem, vmem),
        scratch_shapes=[
            pltpu.VMEM((slots, width), BF16),
            pltpu.VMEM((slots, width), BF16),
            pltpu.VMEM((rows, width), BF16),
            pltpu.VMEM((rows, width), BF16),
            pltpu.VMEM((rows, width), BF16),
            pltpu.VMEM((rows, width), BF16),
            pltpu.VMEM((rows, width), BF16),
            pltpu.VMEM((rows, width), F32),
            pltpu.VMEM((rows, width), BF16),
            pltpu.VMEM((slots, width), BF16),
            pltpu.VMEM((slots, width), BF16),
            pltpu.VMEM((devices, 1, rows), F32),
            pltpu.VMEM((128, rows), F32),
            pltpu.VMEM((rows, 1), F32),
            pltpu.VMEM((rows, 1), F32),
            pltpu.VMEM((rows, 1), F32),
            pltpu.VMEM((rows, 1), F32),
            pltpu.VMEM((rows, 1), F32),
            pltpu.VMEM((1, rows), jnp.int32),
            dma((2,)),
            dma((devices,)),
            dma((devices,)),
            dma((4,)),
            dma((4,)),
            dma((devices,)),
            dma((devices,)),
            dma((devices,)),
            dma((devices,)),
        ],
        compiler_params=pltpu.CompilerParams(
            collective_id=0, has_side_effects=True, vmem_limit_bytes=48 * 1024 * 1024
        ),
    )(
        embeddings,
        position.reshape(1, rows),
        member.reshape(1, rows),
        cluster.reshape(devices, 1, rows),
    )
    return smoothed, counts.reshape(rows).astype(BF16)


def solution(mesh):
    in_specs = (P(("groups", "blk"), None), P(("groups", "blk")), P(("groups", "blk")), P("groups"))
    out_specs = (P(("groups", "blk"), None), P(("groups", "blk")))
    return jax.shard_map(local, mesh=mesh, in_specs=in_specs, out_specs=out_specs, check_vma=False)
```

```python
import functools

import jax
import jax.numpy as jnp
from jax import lax
from jax.experimental import pallas as pl
from jax.experimental.pallas import tpu as pltpu
from jax.sharding import PartitionSpec as P

SHARPNESS = 32.0
EPSILON = 1e-06
TILE = 256
CHUNKS = 4
F32 = jnp.float32
BF16 = jnp.bfloat16


def snake(device, devices):
    if devices != 16:
        return device
    z, y, core = device // 4, (device // 2) % 2, device % 2
    turn = z % 2
    return z * 4 + (y + turn - 2 * y * turn) * 2 + core


def as_column(row):
    return jnp.transpose(jnp.broadcast_to(row, (128, row.shape[1])))[:, :1]


def as_row(column):
    return jnp.transpose(jnp.broadcast_to(column, (column.shape[0], 128)))[:1, :]


def ones_where(condition):
    return jnp.where(condition, 1.0, 0.0)


def kernel(
    devices, slab, emb_hbm, pos, mem, ids, out, count_out,
    emb, outgoing, incoming, win, weights, returning, returned,
    send_pick, restore_pick, place_pick, return_pick,
    tallies, tally_table, own_inv, own_ids, tally, mem_in,
    emb_sem, mem_sems, out_send, out_recv, win_send, win_recv, back_send, back_recv,
    tal_send, tal_recv,
):
    rows, width = emb.shape
    slots = devices * slab
    per_peer = rows // devices
    piece = width // CHUNKS
    me = lax.axis_index("blk")
    block = snake(me, devices)
    chip, core = block // 2, block % 2
    chips = devices // 2

    def dev(b):
        return {"blk": b}

    def remote(src, dst, send, recv, target):
        return pltpu.make_async_remote_copy(
            src_ref=src, dst_ref=dst, send_sem=send, recv_sem=recv,
            device_id=dev(target), device_id_type=pl.DeviceIdType.MESH,
        )

    def columns(c):
        return pl.ds(c * piece, piece)

    def at_slab(ref, index, c):
        return ref.at[pl.ds(pl.multiple_of(index * slab, slab), slab), columns(c)]

    def in_tiles(count):
        def run(body):
            @pl.loop(0, count // TILE)
            def _(t):
                start = pl.multiple_of(t * TILE, TILE)
                body(start, pl.ds(start, TILE))
        return run

    def permute(pick, source, target, c):
        @in_tiles(target.shape[0])
        def _(start, part):
            target[part, columns(c)] = jnp.dot(
                pick[part, :], source[:, columns(c)], preferred_element_type=F32
            ).astype(BF16)

    def make_picks(to_slot, from_slot, slot_row):
        slot_col = as_column(slot_row)
        places = lax.broadcasted_iota(jnp.int32, (slots, rows), 0).astype(F32)
        to_slot[...] = ones_where(places == slot_row).astype(BF16)
        lanes = lax.broadcasted_iota(jnp.int32, (rows, slots), 1).astype(F32)
        from_slot[...] = ones_where(lanes == slot_col).astype(BF16)

    fetch = pltpu.make_async_copy(emb_hbm, emb, emb_sem)
    fetch.start()
    barrier = pltpu.get_barrier_semaphore()

    @pl.loop(1, devices)
    def _(k):
        pl.semaphore_signal(
            barrier, inc=1, device_id=dev((me + k) % devices),
            device_id_type=pl.DeviceIdType.MESH,
        )

    pos_row = pos[...].astype(F32)
    pos_col = as_column(pos_row)
    rank = jnp.sum(ones_where(pos_col < pos_row), axis=0, keepdims=True)
    block_row = lax.shift_right_logical(pos[...], (rows - 1).bit_length()).astype(F32)
    send_row = rank + block_row * (slab - per_peer)
    make_picks(send_pick, restore_pick, send_row)
    fetch.wait()
    permute(send_pick, emb, outgoing, 0)
    pl.semaphore_wait(barrier, devices - 1)

    def out_copy(k, c):
        peer = (me + k) % devices
        return remote(
            at_slab(outgoing, snake(peer, devices), c), at_slab(incoming, me, c),
            out_send.at[c, k], out_recv.at[c, k], peer,
        )

    def mem_copy():
        return remote(mem, mem_in, mem_sems.at[0], mem_sems.at[1], block)

    @pl.when(block != me)
    def _():
        mem_copy().start()

    for c in range(CHUNKS):
        if c > 0:
            permute(send_pick, emb, outgoing, c)

        @pl.loop(1, devices)
        def _(k):
            out_copy(k, c).start()

        at_slab(incoming, me, c)[...] = at_slab(outgoing, block, c)[...]

    @pl.when(block == me)
    def _():
        mem_in[...] = mem[...]

    @pl.when(block != me)
    def _():
        mem_copy().wait()

    src_row = lax.shift_right_logical(mem_in[...], (rows - 1).bit_length()).astype(F32)
    src_col = as_column(src_row)
    earlier = lax.broadcasted_iota(jnp.int32, (rows, rows), 0) < lax.broadcasted_iota(
        jnp.int32, (rows, rows), 1
    )
    before = jnp.sum(ones_where((src_col == src_row) & earlier), axis=0, keepdims=True)
    make_picks(return_pick, place_pick, src_row * slab + before)
    own_ids[...] = as_column(ids[block].astype(F32))

    mate_dev = snake(block + 1 - 2 * core, devices)
    has_prev, has_after = chip > 0, chip < chips - 1
    prev_dev = snake(jnp.maximum(block - 2, 0), devices)
    after_dev = snake(jnp.minimum(block + 2, devices - 1), devices)
    own, mate, prev, after, relayed = (win.at[pl.ds(j * rows, rows)] for j in range(5))

    def window_copy(source, target, way, c, device):
        return remote(
            source.at[:, columns(c)], target.at[:, columns(c)],
            win_send.at[way, c], win_recv.at[way, c], device,
        )

    def to_mate(c):
        return window_copy(own, mate, 0, c, mate_dev)

    def to_after(c):
        return window_copy(own, prev, 1, c, after_dev)

    def to_prev(c):
        return window_copy(own, after, 2, c, prev_dev)

    def relay(source, c):
        return window_copy(source, relayed, 3, c, mate_dev)

    for c in range(CHUNKS):
        @pl.loop(1, devices)
        def _(k):
            out_copy(k, c).wait_recv()

        permute(place_pick, incoming, own, c)

        @pl.when(has_after)
        def _():
            to_after(c).start()

        @pl.when(has_prev)
        def _():
            to_prev(c).start()

        to_mate(c).start()

    def inverse(ref):
        widened = ref[...].astype(F32)
        return lax.rsqrt(jnp.sum(widened * widened, axis=1, keepdims=True) + EPSILON)

    def visit(j, other, other_inv, other_block):
        other_ids = ids[other_block].astype(F32)
        other_inv_row = as_row(other_inv)

        @in_tiles(rows)
        def _(start, part):
            products = lax.dot_general(
                own[part, :], other[...], (((1,), (1,)), ((), ())), preferred_element_type=F32
            )
            half = products * (own_inv[part, :] * (0.5 * SHARPNESS)) * other_inv_row
            allowed = own_ids[part, :] == other_ids
            if j == 0:
                here = lax.broadcasted_iota(jnp.int32, (TILE, rows), 0) + start
                there = lax.broadcasted_iota(jnp.int32, (TILE, rows), 1)
                allowed = allowed & (here != there)
            scores = jnp.where(allowed, 0.5 + 0.5 * jnp.tanh(half), 0.0)
            weights[part, pl.ds(j * rows, rows)] = scores.astype(BF16)
            counted = jnp.sum(scores, axis=1, keepdims=True)
            if j == 0:
                tally[part, :] = counted
            else:
                tally[part, :] += counted

    def absent(j, other):
        other[...] = jnp.zeros_like(other)
        weights[:, pl.ds(j * rows, rows)] = jnp.zeros((rows, rows), BF16)

    gets_relay = ((core == 0) & has_prev) | ((core == 1) & has_after)

    own_inv[...] = inverse(own)
    visit(0, own, own_inv[...], block)

    for missing, j, ref in (
        (chip == 0, 2, prev),
        (chip == chips - 1, 3, after),
        (((core == 0) & (chip == 0)) | ((core == 1) & (chip == chips - 1)), 4, relayed),
    ):
        @pl.when(missing)
        def _():
            absent(j, ref)

    for c in range(CHUNKS):
        to_mate(c).wait_recv()

    visit(1, mate, inverse(mate), block + 1 - 2 * core)

    for c in range(CHUNKS):
        @pl.when(has_prev)
        def _():
            to_after(c).wait_recv()

            @pl.when(core == 1)
            def _():
                relay(prev, c).start()

        @pl.when(has_after)
        def _():
            to_prev(c).wait_recv()

            @pl.when(core == 0)
            def _():
                relay(after, c).start()

    @pl.when(has_prev)
    def _():
        visit(2, prev, inverse(prev), block - 2)

    @pl.when(has_after)
    def _():
        visit(3, after, inverse(after), block + 2)

    @pl.when(gets_relay)
    def _():
        for c in range(CHUNKS):
            relay(prev, c).wait_recv()

        visit(4, relayed, inverse(relayed), block - 1 + 2 * core)

    tallies[block] = as_row(tally[...])

    def tally_copy(k):
        peer = (me + k) % devices
        return remote(
            tallies.at[block], tallies.at[block], tal_send.at[k], tal_recv.at[k], peer
        )

    def back_copy(k, c):
        peer = (me + k) % devices
        return remote(
            at_slab(returning, peer, c), at_slab(returned, block, c),
            back_send.at[c, k], back_recv.at[c, k], peer,
        )

    for c in range(CHUNKS):
        @in_tiles(rows)
        def _(start, part):
            totals = jnp.dot(weights[part, :], win[:, columns(c)], preferred_element_type=F32)
            emb[part, columns(c)] = (totals * lax.rsqrt(1.0 + tally[part, :])).astype(BF16)

        permute(return_pick, emb, returning, c)

        @pl.loop(1, devices)
        def _(k):
            back_copy(k, c).start()

        at_slab(returned, block, c)[...] = at_slab(returning, me, c)[...]

    @pl.loop(1, devices)
    def _(k):
        tally_copy(k).start()

    @pl.loop(1, devices)
    def _(k):
        tally_copy(k).wait_recv()

    tally_table[...] = jnp.zeros_like(tally_table)

    @pl.loop(0, devices)
    def _(b):
        tally_table[pl.ds(b, 1), :] = tallies[b]

    which = lax.broadcasted_iota(jnp.int32, (128, rows), 0).astype(F32)
    in_block = jnp.dot(
        jnp.transpose(tally_table[...]).astype(BF16),
        ones_where(which == block_row).astype(BF16),
        preferred_element_type=F32,
    )
    inside = pos_row - block_row * rows
    lines = lax.broadcasted_iota(jnp.int32, (rows, rows), 0).astype(F32)
    count_out[...] = jnp.sum(jnp.where(lines == inside, in_block, 0.0), axis=0, keepdims=True)

    for c in range(CHUNKS):
        @pl.loop(1, devices)
        def _(k):
            back_copy(k, c).wait_recv()

        permute(restore_pick, returned, out, c)

    @pl.loop(1, devices)
    def _(k):
        tally_copy(k).wait_send()
        for c in range(CHUNKS):
            out_copy(k, c).wait_send()
            back_copy(k, c).wait_send()

    for c in range(CHUNKS):
        to_mate(c).wait_send()

        @pl.when(has_after)
        def _():
            to_after(c).wait_send()

        @pl.when(has_prev)
        def _():
            to_prev(c).wait_send()

        @pl.when(((core == 1) & has_prev) | ((core == 0) & has_after))
        def _():
            relay(prev, c).wait_send()


def local(embeddings, position, member, cluster):
    rows, width = embeddings.shape
    devices = lax.axis_size("blk")
    slab = max(16, rows // devices)
    slots = devices * slab
    vmem = pl.BlockSpec(memory_space=pltpu.VMEM)
    dma = pltpu.SemaphoreType.DMA
    smoothed, counts = pl.pallas_call(
        functools.partial(kernel, devices, slab),
        out_shape=(
            jax.ShapeDtypeStruct((rows, width), BF16),
            jax.ShapeDtypeStruct((1, rows), F32),
        ),
        in_specs=[pl.BlockSpec(memory_space=pl.ANY), vmem, vmem, vmem],
        out_specs=(vmem, vmem),
        scratch_shapes=[
            pltpu.VMEM((rows, width), BF16),
            pltpu.VMEM((slots, width), BF16),
            pltpu.VMEM((slots, width), BF16),
            pltpu.VMEM((5 * rows, width), BF16),
            pltpu.VMEM((rows, 5 * rows), BF16),
            pltpu.VMEM((slots, width), BF16),
            pltpu.VMEM((slots, width), BF16),
            pltpu.VMEM((slots, rows), BF16),
            pltpu.VMEM((rows, slots), BF16),
            pltpu.VMEM((rows, slots), BF16),
            pltpu.VMEM((slots, rows), BF16),
            pltpu.VMEM((devices, 1, rows), F32),
            pltpu.VMEM((128, rows), F32),
            pltpu.VMEM((rows, 1), F32),
            pltpu.VMEM((rows, 1), F32),
            pltpu.VMEM((rows, 1), F32),
            pltpu.VMEM((1, rows), jnp.int32),
            dma,
            dma((2,)),
            dma((CHUNKS, devices)),
            dma((CHUNKS, devices)),
            dma((4, CHUNKS)),
            dma((4, CHUNKS)),
            dma((CHUNKS, devices)),
            dma((CHUNKS, devices)),
            dma((devices,)),
            dma((devices,)),
        ],
        compiler_params=pltpu.CompilerParams(
            collective_id=0, has_side_effects=True, vmem_limit_bytes=48 * 1024 * 1024
        ),
    )(
        embeddings,
        position.reshape(1, rows),
        member.reshape(1, rows),
        cluster.reshape(devices, 1, rows),
    )
    return smoothed, counts.reshape(rows).astype(BF16)


def solution(mesh):
    in_specs = (P(("groups", "blk"), None), P(("groups", "blk")), P(("groups", "blk")), P("groups"))
    out_specs = (P(("groups", "blk"), None), P(("groups", "blk")))
    return jax.shard_map(local, mesh=mesh, in_specs=in_specs, out_specs=out_specs, check_vma=False)
```

```python
import functools

import jax
import jax.numpy as jnp
from jax import lax
from jax.experimental import pallas as pl
from jax.experimental.pallas import tpu as pltpu
from jax.sharding import PartitionSpec as P

SHARPNESS = 32.0
EPSILON = 1e-06
TILE = 512
CHUNKS = 2
F32 = jnp.float32
BF16 = jnp.bfloat16


def snake(device, devices):
    if devices != 16:
        return device
    z, y, core = device // 4, (device // 2) % 2, device % 2
    turn = z % 2
    return z * 4 + (y + turn - 2 * y * turn) * 2 + core


def as_column(row):
    return jnp.transpose(jnp.broadcast_to(row, (128, row.shape[1])))[:, :1]


def as_row(column):
    return jnp.transpose(jnp.broadcast_to(column, (column.shape[0], 128)))[:1, :]


def ones_where(condition):
    return jnp.where(condition, 1.0, 0.0)


def kernel(
    devices, slab, emb_hbm, pos, mem, ids, out, count_out,
    emb, outgoing, incoming, win, weights, returning, returned,
    send_pick, restore_pick, place_pick, return_pick,
    tallies, tally_table, own_inv, own_ids, tally, mem_in,
    emb_sem, mem_sems, out_send, out_recv, win_send, win_recv, back_send, back_recv,
    tal_send, tal_recv,
):
    rows, width = emb.shape
    slots = devices * slab
    per_peer = rows // devices
    piece = width // CHUNKS
    me = lax.axis_index("blk")
    block = snake(me, devices)
    chip, core = block // 2, block % 2
    chips = devices // 2

    def dev(b):
        return {"blk": b}

    def remote(src, dst, send, recv, target):
        return pltpu.make_async_remote_copy(
            src_ref=src, dst_ref=dst, send_sem=send, recv_sem=recv,
            device_id=dev(target), device_id_type=pl.DeviceIdType.MESH,
        )

    def columns(c):
        return pl.ds(c * piece, piece)

    def at_slab(ref, index, c):
        return ref.at[pl.ds(pl.multiple_of(index * slab, slab), slab), columns(c)]

    def in_tiles(count):
        def run(body):
            @pl.loop(0, count // TILE)
            def _(t):
                start = pl.multiple_of(t * TILE, TILE)
                body(start, pl.ds(start, TILE))
        return run

    def permute(pick, source, target, c):
        @in_tiles(target.shape[0])
        def _(start, part):
            target[part, columns(c)] = jnp.dot(
                pick[part, :], source[:, columns(c)], preferred_element_type=F32
            ).astype(BF16)

    def make_picks(to_slot, from_slot, slot_row):
        slot_col = as_column(slot_row)
        places = lax.broadcasted_iota(jnp.int32, (slots, rows), 0).astype(F32)
        to_slot[...] = ones_where(places == slot_row).astype(BF16)
        lanes = lax.broadcasted_iota(jnp.int32, (rows, slots), 1).astype(F32)
        from_slot[...] = ones_where(lanes == slot_col).astype(BF16)

    fetch = pltpu.make_async_copy(emb_hbm, emb, emb_sem)
    fetch.start()
    barrier = pltpu.get_barrier_semaphore()

    @pl.loop(1, devices)
    def _(k):
        pl.semaphore_signal(
            barrier, inc=1, device_id=dev((me + k) % devices),
            device_id_type=pl.DeviceIdType.MESH,
        )

    pos_row = pos[...].astype(F32)
    pos_col = as_column(pos_row)
    rank = jnp.sum(ones_where(pos_col < pos_row), axis=0, keepdims=True)
    block_row = lax.shift_right_logical(pos[...], (rows - 1).bit_length()).astype(F32)
    send_row = rank + block_row * (slab - per_peer)
    make_picks(send_pick, restore_pick, send_row)
    fetch.wait()
    permute(send_pick, emb, outgoing, 0)
    pl.semaphore_wait(barrier, devices - 1)

    def out_copy(k, c):
        peer = (me + k) % devices
        return remote(
            at_slab(outgoing, snake(peer, devices), c), at_slab(incoming, me, c),
            out_send.at[c, k], out_recv.at[c, k], peer,
        )

    def mem_copy():
        return remote(mem, mem_in, mem_sems.at[0], mem_sems.at[1], block)

    @pl.when(block != me)
    def _():
        mem_copy().start()

    for c in range(CHUNKS):
        if c > 0:
            permute(send_pick, emb, outgoing, c)

        @pl.loop(1, devices)
        def _(k):
            out_copy(k, c).start()

        at_slab(incoming, me, c)[...] = at_slab(outgoing, block, c)[...]

    @pl.when(block == me)
    def _():
        mem_in[...] = mem[...]

    @pl.when(block != me)
    def _():
        mem_copy().wait()

    src_row = lax.shift_right_logical(mem_in[...], (rows - 1).bit_length()).astype(F32)
    src_col = as_column(src_row)
    earlier = lax.broadcasted_iota(jnp.int32, (rows, rows), 0) < lax.broadcasted_iota(
        jnp.int32, (rows, rows), 1
    )
    before = jnp.sum(ones_where((src_col == src_row) & earlier), axis=0, keepdims=True)
    make_picks(return_pick, place_pick, src_row * slab + before)
    own_ids[...] = as_column(ids[block].astype(F32))

    mate_dev = snake(block + 1 - 2 * core, devices)
    has_prev, has_after = chip > 0, chip < chips - 1
    prev_dev = snake(jnp.maximum(block - 2, 0), devices)
    after_dev = snake(jnp.minimum(block + 2, devices - 1), devices)
    own, mate, prev, after, relayed = (win.at[pl.ds(j * rows, rows)] for j in range(5))

    def window_copy(source, target, way, c, device):
        return remote(
            source.at[:, columns(c)], target.at[:, columns(c)],
            win_send.at[way, c], win_recv.at[way, c], device,
        )

    def to_mate(c):
        return window_copy(own, mate, 0, c, mate_dev)

    def to_after(c):
        return window_copy(own, prev, 1, c, after_dev)

    def to_prev(c):
        return window_copy(own, after, 2, c, prev_dev)

    def relay(source, c):
        return window_copy(source, relayed, 3, c, mate_dev)

    for c in range(CHUNKS):
        @pl.loop(1, devices)
        def _(k):
            out_copy(k, c).wait_recv()

        permute(place_pick, incoming, own, c)

        @pl.when(has_after)
        def _():
            to_after(c).start()

        @pl.when(has_prev)
        def _():
            to_prev(c).start()

        to_mate(c).start()

    def inverse(ref):
        widened = ref[...].astype(F32)
        return lax.rsqrt(jnp.sum(widened * widened, axis=1, keepdims=True) + EPSILON)

    def visit(j, other, other_inv, other_block):
        other_ids = ids[other_block].astype(F32)
        other_inv_row = as_row(other_inv)

        @in_tiles(rows)
        def _(start, part):
            products = lax.dot_general(
                own[part, :], other[...], (((1,), (1,)), ((), ())), preferred_element_type=F32
            )
            half = products * (own_inv[part, :] * (0.5 * SHARPNESS)) * other_inv_row
            allowed = own_ids[part, :] == other_ids
            if j == 0:
                here = lax.broadcasted_iota(jnp.int32, (TILE, rows), 0) + start
                there = lax.broadcasted_iota(jnp.int32, (TILE, rows), 1)
                allowed = allowed & (here != there)
            scores = jnp.where(allowed, 0.5 + 0.5 * jnp.tanh(half), 0.0)
            weights[part, pl.ds(j * rows, rows)] = scores.astype(BF16)
            counted = jnp.sum(scores, axis=1, keepdims=True)
            if j == 0:
                tally[part, :] = counted
            else:
                tally[part, :] += counted

    def absent(j, other):
        other[...] = jnp.zeros_like(other)
        weights[:, pl.ds(j * rows, rows)] = jnp.zeros((rows, rows), BF16)

    gets_relay = ((core == 0) & has_prev) | ((core == 1) & has_after)

    own_inv[...] = inverse(own)
    visit(0, own, own_inv[...], block)

    for missing, j, ref in (
        (chip == 0, 2, prev),
        (chip == chips - 1, 3, after),
        (((core == 0) & (chip == 0)) | ((core == 1) & (chip == chips - 1)), 4, relayed),
    ):
        @pl.when(missing)
        def _():
            absent(j, ref)

    for c in range(CHUNKS):
        to_mate(c).wait_recv()

    visit(1, mate, inverse(mate), block + 1 - 2 * core)

    for c in range(CHUNKS):
        @pl.when(has_prev)
        def _():
            to_after(c).wait_recv()

            @pl.when(core == 1)
            def _():
                relay(prev, c).start()

        @pl.when(has_after)
        def _():
            to_prev(c).wait_recv()

            @pl.when(core == 0)
            def _():
                relay(after, c).start()

    @pl.when(has_prev)
    def _():
        visit(2, prev, inverse(prev), block - 2)

    @pl.when(has_after)
    def _():
        visit(3, after, inverse(after), block + 2)

    @pl.when(gets_relay)
    def _():
        for c in range(CHUNKS):
            relay(prev, c).wait_recv()

        visit(4, relayed, inverse(relayed), block - 1 + 2 * core)

    tallies[block] = as_row(tally[...])

    def tally_copy(k):
        peer = (me + k) % devices
        return remote(
            tallies.at[block], tallies.at[block], tal_send.at[k], tal_recv.at[k], peer
        )

    def back_copy(k, c):
        peer = (me + k) % devices
        return remote(
            at_slab(returning, peer, c), at_slab(returned, block, c),
            back_send.at[c, k], back_recv.at[c, k], peer,
        )

    for c in range(CHUNKS):
        @in_tiles(rows)
        def _(start, part):
            totals = jnp.dot(weights[part, :], win[:, columns(c)], preferred_element_type=F32)
            emb[part, columns(c)] = (totals * lax.rsqrt(1.0 + tally[part, :])).astype(BF16)

        permute(return_pick, emb, returning, c)

        @pl.loop(1, devices)
        def _(k):
            back_copy(k, c).start()

        at_slab(returned, block, c)[...] = at_slab(returning, me, c)[...]

    @pl.loop(1, devices)
    def _(k):
        tally_copy(k).start()

    @pl.loop(1, devices)
    def _(k):
        tally_copy(k).wait_recv()

    tally_table[...] = jnp.zeros_like(tally_table)

    @pl.loop(0, devices)
    def _(b):
        tally_table[pl.ds(b, 1), :] = tallies[b]

    which = lax.broadcasted_iota(jnp.int32, (128, rows), 0).astype(F32)
    in_block = jnp.dot(
        jnp.transpose(tally_table[...]).astype(BF16),
        ones_where(which == block_row).astype(BF16),
        preferred_element_type=F32,
    )
    inside = pos_row - block_row * rows
    lines = lax.broadcasted_iota(jnp.int32, (rows, rows), 0).astype(F32)
    count_out[...] = jnp.sum(jnp.where(lines == inside, in_block, 0.0), axis=0, keepdims=True)

    for c in range(CHUNKS):
        @pl.loop(1, devices)
        def _(k):
            back_copy(k, c).wait_recv()

        permute(restore_pick, returned, out, c)

    @pl.loop(1, devices)
    def _(k):
        tally_copy(k).wait_send()
        for c in range(CHUNKS):
            out_copy(k, c).wait_send()
            back_copy(k, c).wait_send()

    for c in range(CHUNKS):
        to_mate(c).wait_send()

        @pl.when(has_after)
        def _():
            to_after(c).wait_send()

        @pl.when(has_prev)
        def _():
            to_prev(c).wait_send()

        @pl.when(((core == 1) & has_prev) | ((core == 0) & has_after))
        def _():
            relay(prev, c).wait_send()


def local(embeddings, position, member, cluster):
    rows, width = embeddings.shape
    devices = lax.axis_size("blk")
    slab = max(16, rows // devices)
    slots = devices * slab
    vmem = pl.BlockSpec(memory_space=pltpu.VMEM)
    dma = pltpu.SemaphoreType.DMA
    smoothed, counts = pl.pallas_call(
        functools.partial(kernel, devices, slab),
        out_shape=(
            jax.ShapeDtypeStruct((rows, width), BF16),
            jax.ShapeDtypeStruct((1, rows), F32),
        ),
        in_specs=[pl.BlockSpec(memory_space=pl.ANY), vmem, vmem, vmem],
        out_specs=(vmem, vmem),
        scratch_shapes=[
            pltpu.VMEM((rows, width), BF16),
            pltpu.VMEM((slots, width), BF16),
            pltpu.VMEM((slots, width), BF16),
            pltpu.VMEM((5 * rows, width), BF16),
            pltpu.VMEM((rows, 5 * rows), BF16),
            pltpu.VMEM((slots, width), BF16),
            pltpu.VMEM((slots, width), BF16),
            pltpu.VMEM((slots, rows), BF16),
            pltpu.VMEM((rows, slots), BF16),
            pltpu.VMEM((rows, slots), BF16),
            pltpu.VMEM((slots, rows), BF16),
            pltpu.VMEM((devices, 1, rows), F32),
            pltpu.VMEM((128, rows), F32),
            pltpu.VMEM((rows, 1), F32),
            pltpu.VMEM((rows, 1), F32),
            pltpu.VMEM((rows, 1), F32),
            pltpu.VMEM((1, rows), jnp.int32),
            dma,
            dma((2,)),
            dma((CHUNKS, devices)),
            dma((CHUNKS, devices)),
            dma((4, CHUNKS)),
            dma((4, CHUNKS)),
            dma((CHUNKS, devices)),
            dma((CHUNKS, devices)),
            dma((devices,)),
            dma((devices,)),
        ],
        compiler_params=pltpu.CompilerParams(
            collective_id=0, has_side_effects=True, vmem_limit_bytes=48 * 1024 * 1024
        ),
    )(
        embeddings,
        position.reshape(1, rows),
        member.reshape(1, rows),
        cluster.reshape(devices, 1, rows),
    )
    return smoothed, counts.reshape(rows).astype(BF16)


def solution(mesh):
    in_specs = (P(("groups", "blk"), None), P(("groups", "blk")), P(("groups", "blk")), P("groups"))
    out_specs = (P(("groups", "blk"), None), P(("groups", "blk")))
    return jax.shard_map(local, mesh=mesh, in_specs=in_specs, out_specs=out_specs, check_vma=False)
```

```python
import functools

import jax
import jax.numpy as jnp
from jax import lax
from jax.experimental import pallas as pl
from jax.experimental.pallas import tpu as pltpu
from jax.sharding import PartitionSpec as P

SHARPNESS = 32.0
EPSILON = 1e-06
TILE = 512
CHUNKS = 2
F32 = jnp.float32
BF16 = jnp.bfloat16


def snake(device, devices):
    if devices != 16:
        return device
    z, y, core = device // 4, (device // 2) % 2, device % 2
    turn = z % 2
    return z * 4 + (y + turn - 2 * y * turn) * 2 + core


def as_column(row):
    return jnp.transpose(jnp.broadcast_to(row, (128, row.shape[1])))[:, :1]


def as_row(column):
    return jnp.transpose(jnp.broadcast_to(column, (column.shape[0], 128)))[:1, :]


def ones_where(condition):
    return jnp.where(condition, 1.0, 0.0)


def kernel(
    devices, slab, emb_hbm, pos, mem, ids, out, count_out,
    emb, outgoing, incoming, win, weights, returning, returned,
    send_pick, restore_pick, place_pick, return_pick,
    tallies, tally_table, own_inv, own_ids, tally, mem_in,
    emb_sem, mem_sems, out_send, out_recv, win_send, win_recv, back_send, back_recv,
    tal_send, tal_recv,
):
    rows, width = emb.shape
    slots = devices * slab
    per_peer = rows // devices
    piece = width // CHUNKS
    me = lax.axis_index("blk")
    block = snake(me, devices)
    chip, core = block // 2, block % 2
    chips = devices // 2

    def dev(b):
        return {"blk": b}

    def remote(src, dst, send, recv, target):
        return pltpu.make_async_remote_copy(
            src_ref=src, dst_ref=dst, send_sem=send, recv_sem=recv,
            device_id=dev(target), device_id_type=pl.DeviceIdType.MESH,
        )

    def columns(c):
        return pl.ds(c * piece, piece)

    def at_slab(ref, index, c):
        return ref.at[pl.ds(pl.multiple_of(index * slab, slab), slab), columns(c)]

    def in_tiles(count):
        def run(body):
            @pl.loop(0, count // TILE)
            def _(t):
                start = pl.multiple_of(t * TILE, TILE)
                body(start, pl.ds(start, TILE))
        return run

    def permute(pick, source, target, c):
        @in_tiles(target.shape[0])
        def _(start, part):
            target[part, columns(c)] = jnp.dot(
                pick[part, :], source[:, columns(c)], preferred_element_type=F32
            ).astype(BF16)

    def make_picks(to_slot, from_slot, slot_row):
        slot_col = as_column(slot_row)
        places = lax.broadcasted_iota(jnp.int32, (slots, rows), 0).astype(F32)
        to_slot[...] = ones_where(places == slot_row).astype(BF16)
        lanes = lax.broadcasted_iota(jnp.int32, (rows, slots), 1).astype(F32)
        from_slot[...] = ones_where(lanes == slot_col).astype(BF16)

    fetch = pltpu.make_async_copy(emb_hbm, emb, emb_sem)
    fetch.start()
    barrier = pltpu.get_barrier_semaphore()

    @pl.loop(1, devices)
    def _(k):
        pl.semaphore_signal(
            barrier, inc=1, device_id=dev((me + k) % devices),
            device_id_type=pl.DeviceIdType.MESH,
        )

    pos_row = pos[...].astype(F32)
    pos_col = as_column(pos_row)
    rank = jnp.sum(ones_where(pos_col < pos_row), axis=0, keepdims=True)
    block_row = lax.shift_right_logical(pos[...], (rows - 1).bit_length()).astype(F32)
    send_row = rank + block_row * (slab - per_peer)
    make_picks(send_pick, restore_pick, send_row)
    fetch.wait()
    permute(send_pick, emb, outgoing, 0)
    pl.semaphore_wait(barrier, devices - 1)

    def out_copy(k, c):
        peer = (me + k) % devices
        return remote(
            at_slab(outgoing, snake(peer, devices), c), at_slab(incoming, me, c),
            out_send.at[c, k], out_recv.at[c, k], peer,
        )

    def mem_copy():
        return remote(mem, mem_in, mem_sems.at[0], mem_sems.at[1], block)

    @pl.when(block != me)
    def _():
        mem_copy().start()

    for c in range(CHUNKS):
        if c > 0:
            permute(send_pick, emb, outgoing, c)

        @pl.loop(1, devices)
        def _(k):
            out_copy(k, c).start()

        at_slab(incoming, me, c)[...] = at_slab(outgoing, block, c)[...]

    @pl.when(block == me)
    def _():
        mem_in[...] = mem[...]

    @pl.when(block != me)
    def _():
        mem_copy().wait()

    src_row = lax.shift_right_logical(mem_in[...], (rows - 1).bit_length()).astype(F32)
    src_col = as_column(src_row)
    earlier = lax.broadcasted_iota(jnp.int32, (rows, rows), 0) < lax.broadcasted_iota(
        jnp.int32, (rows, rows), 1
    )
    before = jnp.sum(ones_where((src_col == src_row) & earlier), axis=0, keepdims=True)
    make_picks(return_pick, place_pick, src_row * slab + before)
    own_ids[...] = as_column(ids[block].astype(F32))

    mate_dev = snake(block + 1 - 2 * core, devices)
    has_prev, has_after = chip > 0, chip < chips - 1
    prev_dev = snake(jnp.maximum(block - 2, 0), devices)
    after_dev = snake(jnp.minimum(block + 2, devices - 1), devices)
    own, mate, prev, after, relayed = (win.at[pl.ds(j * rows, rows)] for j in range(5))

    def window_copy(source, target, way, c, device):
        return remote(
            source.at[:, columns(c)], target.at[:, columns(c)],
            win_send.at[way, c], win_recv.at[way, c], device,
        )

    def to_mate(c):
        return window_copy(own, mate, 0, c, mate_dev)

    def to_after(c):
        return window_copy(own, prev, 1, c, after_dev)

    def to_prev(c):
        return window_copy(own, after, 2, c, prev_dev)

    def relay(source, c):
        return window_copy(source, relayed, 3, c, mate_dev)

    for c in range(CHUNKS):
        @pl.loop(1, devices)
        def _(k):
            out_copy(k, c).wait_recv()

        permute(place_pick, incoming, own, c)

        @pl.when(has_after)
        def _():
            to_after(c).start()

        @pl.when(has_prev)
        def _():
            to_prev(c).start()

        to_mate(c).start()

    def inverse(ref):
        widened = ref[...].astype(F32)
        return lax.rsqrt(jnp.sum(widened * widened, axis=1, keepdims=True) + EPSILON)

    def visit(j, other, other_inv, other_block):
        other_ids = ids[other_block].astype(F32)
        other_inv_row = as_row(other_inv)

        @in_tiles(rows)
        def _(start, part):
            products = lax.dot_general(
                own[part, :], other[...], (((1,), (1,)), ((), ())), preferred_element_type=F32
            )
            half = products * (own_inv[part, :] * (0.5 * SHARPNESS)) * other_inv_row
            allowed = own_ids[part, :] == other_ids
            if j == 0:
                here = lax.broadcasted_iota(jnp.int32, (TILE, rows), 0) + start
                there = lax.broadcasted_iota(jnp.int32, (TILE, rows), 1)
                allowed = allowed & (here != there)
            scores = jnp.where(allowed, 0.5 + 0.5 * jnp.tanh(half), 0.0)
            weights[part, pl.ds(j * rows, rows)] = scores.astype(BF16)
            counted = jnp.sum(scores, axis=1, keepdims=True)
            if j == 0:
                tally[part, :] = counted
            else:
                tally[part, :] += counted

    def absent(j, other):
        other[...] = jnp.zeros_like(other)
        weights[:, pl.ds(j * rows, rows)] = jnp.zeros((rows, rows), BF16)

    gets_relay = ((core == 0) & has_prev) | ((core == 1) & has_after)

    own_inv[...] = inverse(own)
    visit(0, own, own_inv[...], block)

    for missing, j, ref in (
        (chip == 0, 2, prev),
        (chip == chips - 1, 3, after),
        (((core == 0) & (chip == 0)) | ((core == 1) & (chip == chips - 1)), 4, relayed),
    ):
        @pl.when(missing)
        def _():
            absent(j, ref)

    for c in range(CHUNKS):
        to_mate(c).wait_recv()

    visit(1, mate, inverse(mate), block + 1 - 2 * core)

    for c in range(CHUNKS):
        @pl.when(has_prev)
        def _():
            to_after(c).wait_recv()

            @pl.when(core == 1)
            def _():
                relay(prev, c).start()

        @pl.when(has_after)
        def _():
            to_prev(c).wait_recv()

            @pl.when(core == 0)
            def _():
                relay(after, c).start()

    @pl.when(has_prev)
    def _():
        visit(2, prev, inverse(prev), block - 2)

    @pl.when(has_after)
    def _():
        visit(3, after, inverse(after), block + 2)

    @pl.when(gets_relay)
    def _():
        for c in range(CHUNKS):
            relay(prev, c).wait_recv()

        visit(4, relayed, inverse(relayed), block - 1 + 2 * core)

    tallies[block] = as_row(tally[...])

    def tally_copy(k):
        peer = (me + k) % devices
        return remote(
            tallies.at[block], tallies.at[block], tal_send.at[k], tal_recv.at[k], peer
        )

    def back_copy(k, c):
        peer = (me + k) % devices
        return remote(
            at_slab(returning, peer, c), at_slab(returned, block, c),
            back_send.at[c, k], back_recv.at[c, k], peer,
        )

    for c in range(CHUNKS):
        @in_tiles(rows)
        def _(start, part):
            totals = jnp.dot(weights[part, :], win[:, columns(c)], preferred_element_type=F32)
            emb[part, columns(c)] = (totals * lax.rsqrt(1.0 + tally[part, :])).astype(BF16)

        permute(return_pick, emb, returning, c)

        @pl.loop(1, devices)
        def _(k):
            back_copy(k, c).start()

        at_slab(returned, block, c)[...] = at_slab(returning, me, c)[...]

    @pl.loop(1, devices)
    def _(k):
        tally_copy(k).start()

    @pl.loop(1, devices)
    def _(k):
        tally_copy(k).wait_recv()

    tally_table[...] = jnp.zeros_like(tally_table)

    @pl.loop(0, devices)
    def _(b):
        tally_table[pl.ds(b, 1), :] = tallies[b]

    which = lax.broadcasted_iota(jnp.int32, (128, rows), 0).astype(F32)
    in_block = jnp.dot(
        jnp.transpose(tally_table[...]).astype(BF16),
        ones_where(which == block_row).astype(BF16),
        preferred_element_type=F32,
    )
    inside = pos_row - block_row * rows
    lines = lax.broadcasted_iota(jnp.int32, (rows, rows), 0).astype(F32)
    count_out[...] = jnp.sum(jnp.where(lines == inside, in_block, 0.0), axis=0, keepdims=True)

    for c in range(CHUNKS):
        @pl.loop(1, devices)
        def _(k):
            back_copy(k, c).wait_recv()

        permute(restore_pick, returned, out, c)

    @pl.loop(1, devices)
    def _(k):
        tally_copy(k).wait_send()
        for c in range(CHUNKS):
            out_copy(k, c).wait_send()
            back_copy(k, c).wait_send()

    for c in range(CHUNKS):
        to_mate(c).wait_send()

        @pl.when(has_after)
        def _():
            to_after(c).wait_send()

        @pl.when(has_prev)
        def _():
            to_prev(c).wait_send()

        @pl.when(((core == 1) & has_prev) | ((core == 0) & has_after))
        def _():
            relay(prev, c).wait_send()


def local(embeddings, position, member, cluster):
    rows, width = embeddings.shape
    devices = lax.axis_size("blk")
    slab = max(16, rows // devices)
    slots = devices * slab
    vmem = pl.BlockSpec(memory_space=pltpu.VMEM)
    dma = pltpu.SemaphoreType.DMA
    smoothed, counts = pl.pallas_call(
        functools.partial(kernel, devices, slab),
        out_shape=(
            jax.ShapeDtypeStruct((rows, width), BF16),
            jax.ShapeDtypeStruct((1, rows), F32),
        ),
        in_specs=[pl.BlockSpec(memory_space=pl.ANY), vmem, vmem, vmem],
        out_specs=(vmem, vmem),
        scratch_shapes=[
            pltpu.VMEM((rows, width), BF16),
            pltpu.VMEM((slots, width), BF16),
            pltpu.VMEM((slots, width), BF16),
            pltpu.VMEM((5 * rows, width), BF16),
            pltpu.VMEM((rows, 5 * rows), BF16),
            pltpu.VMEM((slots, width), BF16),
            pltpu.VMEM((slots, width), BF16),
            pltpu.VMEM((slots, rows), BF16),
            pltpu.VMEM((rows, slots), BF16),
            pltpu.VMEM((rows, slots), BF16),
            pltpu.VMEM((slots, rows), BF16),
            pltpu.VMEM((devices, 1, rows), F32),
            pltpu.VMEM((128, rows), F32),
            pltpu.VMEM((rows, 1), F32),
            pltpu.VMEM((rows, 1), F32),
            pltpu.VMEM((rows, 1), F32),
            pltpu.VMEM((1, rows), jnp.int32),
            dma,
            dma((2,)),
            dma((CHUNKS, devices)),
            dma((CHUNKS, devices)),
            dma((4, CHUNKS)),
            dma((4, CHUNKS)),
            dma((CHUNKS, devices)),
            dma((CHUNKS, devices)),
            dma((devices,)),
            dma((devices,)),
        ],
        compiler_params=pltpu.CompilerParams(
            collective_id=0, has_side_effects=True, vmem_limit_bytes=63 * 1024 * 1024
        ),
    )(
        embeddings,
        position.reshape(1, rows),
        member.reshape(1, rows),
        cluster.reshape(devices, 1, rows),
    )
    return smoothed, counts.reshape(rows).astype(BF16)


def solution(mesh):
    in_specs = (P(("groups", "blk"), None), P(("groups", "blk")), P(("groups", "blk")), P("groups"))
    out_specs = (P(("groups", "blk"), None), P(("groups", "blk")))
    return jax.shard_map(local, mesh=mesh, in_specs=in_specs, out_specs=out_specs, check_vma=False)
```
